512 devices in a mesh: seq: 64 (over z_lo, y, x), res: 8 (over z_hi, core).
Axes of the slice: x: 4, y: 8, z: 8 (z_hi: 4, z_lo: 2; z = z_hi * 2 + z_lo), core: 2. Of those that a mesh axis runs over, the one named last changes fastest.
Arguments:
- alignment_tensor: bfloat16 [256, 1024, 256], P('seq', 'res'), may hold values from -6 to 6
- scaling_entries: float32 [256], replicated, may hold values from 0.1 to 1.9
- probe_matrix: bfloat16 [256, 256], replicated, may hold values from -0.375 to 0.375
- lookup_matrix: bfloat16 [256, 256], replicated, may hold values from -0.75 to 0.75
- content_matrix: bfloat16 [256, 256], replicated, may hold values from -0.375 to 0.375
- gating_matrix: bfloat16 [256, 256], replicated, may hold values from -0.375 to 0.375
- final_projection_matrix: bfloat16 [256, 256], replicated, may hold values from -1.5 to 1.5
- residue_offset_logits: bfloat16 [8, 1024, 1024], P(None, 'res', 'seq'), may hold values from -10 to 250
Outputs:
- update: bfloat16 [256, 1024, 256], P('seq', 'res')
The draws below stay inside these ranges and needn't reach their ends.
All inputs are finite; a program needn't handle non-finite values.
Results may differ from the reference program's by a relative error of at most 0.012.
Values may be sent and summed in bfloat16 or wider, within the bound.
A program may use at most 64 MiB of HBM per device.

```python
import jax
import jax.numpy as jnp
from jax import lax

FEATURE_DEPTH = 256
HEADS = 8
HEAD = 32
ALIGNED_HOMOLOGS = 256
AMINO_SPAN = 1024


def draw_residue_offset_logits(key, part):
    key = jax.random.fold_in(key, 11)
    keys_all = jax.random.split(key, 7)
    full_shape = (HEADS, AMINO_SPAN, AMINO_SPAN)
    row_offset = jax.random.uniform(keys_all[6], (HEADS, AMINO_SPAN, 1), jnp.float32, -4.0, 4.0)
    noise = jax.random.normal(keys_all[0], full_shape, jnp.float32)
    base = jnp.clip(noise + row_offset, -10.0, 10.0)
    return base.astype(jnp.bfloat16)


def block_levels(stream_key, dims, shards, low, largest):
    def one(dim, blocks):
        heights = jax.random.uniform(jax.random.fold_in(jax.random.fold_in(stream_key, 6), dim), (blocks,), jnp.float32, low / len(shards), largest / len(shards))
        return jnp.repeat(jnp.exp(heights), dims[dim] // blocks).reshape((-1,) + (1,) * (len(dims) - dim - 1))

    gain = one(*shards[0])
    for cut in shards[1:]:
        gain = gain * one(*cut)
    return gain


def centred(stream_key, dims, width, most, pieces=(), kind=jnp.bfloat16):
    array = width * jax.random.normal(stream_key, dims, jnp.float32)
    if pieces:
        array = array * block_levels(stream_key, dims, pieces, -0.22, 0.18)
    return jnp.clip(array, -most, most).astype(kind)


def setup_inputs(seed: int = 0) -> dict:
    arg_keys = jax.random.split(jax.random.key(seed), 9)
    alignment_tensor = centred(arg_keys[0], (ALIGNED_HOMOLOGS, AMINO_SPAN, FEATURE_DEPTH), 1.0, 6.0, ((0, 64), (1, 8)))
    scaling_entries = jnp.clip(1.0 + 0.18 * jax.random.normal(arg_keys[1], (FEATURE_DEPTH,), jnp.float32), 0.1, 1.9)
    probe_matrix = centred(arg_keys[2], (FEATURE_DEPTH, FEATURE_DEPTH), FEATURE_DEPTH ** -0.5, 0.375)
    lookup_matrix = centred(arg_keys[3], (FEATURE_DEPTH, FEATURE_DEPTH), (FEATURE_DEPTH // 4) ** -0.5, 0.75)
    content_matrix = centred(arg_keys[4], (FEATURE_DEPTH, FEATURE_DEPTH), FEATURE_DEPTH ** -0.5, 0.375)
    gating_matrix = centred(arg_keys[5], (FEATURE_DEPTH, FEATURE_DEPTH), FEATURE_DEPTH ** -0.5, 0.375)
    final_projection_matrix = centred(arg_keys[6], (FEATURE_DEPTH, FEATURE_DEPTH), (FEATURE_DEPTH // 16) ** -0.5, 1.5)
    residue_offset_logits = draw_residue_offset_logits(jax.random.fold_in(arg_keys[8], 71), 0)
    return dict(alignment_tensor=alignment_tensor, scaling_entries=scaling_entries, probe_matrix=probe_matrix, lookup_matrix=lookup_matrix, content_matrix=content_matrix, gating_matrix=gating_matrix, final_projection_matrix=final_projection_matrix, residue_offset_logits=residue_offset_logits)


def standardize_features(alignment_tensor, scaling_entries):
    content_entries = alignment_tensor.astype(jnp.float32)
    center = lax.optimization_barrier(jnp.mean(content_entries, axis=-1, keepdims=True))
    variance = lax.optimization_barrier(jnp.mean((content_entries - center) ** 2, axis=-1, keepdims=True))
    return ((content_entries - center) * lax.rsqrt(variance + 1e-05) * scaling_entries).astype(jnp.bfloat16)

def reference(alignment_tensor, scaling_entries, probe_matrix, lookup_matrix, content_matrix, gating_matrix, final_projection_matrix, residue_offset_logits):
    standardized_alignment = standardize_features(alignment_tensor, scaling_entries)
    bias_full = residue_offset_logits.astype(jnp.float32)

    def attend_row(seq_rows):
        queries = (jnp.dot(seq_rows, probe_matrix, preferred_element_type=jnp.float32) * HEAD ** (-0.5)).astype(jnp.bfloat16)
        keys = jnp.dot(seq_rows, lookup_matrix, preferred_element_type=jnp.float32).astype(jnp.bfloat16)
        content_entries = jnp.dot(seq_rows, content_matrix, preferred_element_type=jnp.float32).astype(jnp.bfloat16)
        sigmoid_factors = jax.nn.sigmoid(jnp.dot(seq_rows, gating_matrix, preferred_element_type=jnp.float32))
        q_heads = queries.reshape(AMINO_SPAN, HEADS, HEAD).astype(jnp.float32)
        k_heads = keys.reshape(AMINO_SPAN, HEADS, HEAD).astype(jnp.float32)
        v_heads = content_entries.reshape(AMINO_SPAN, HEADS, HEAD).astype(jnp.float32)
        scores = jnp.einsum('ihd,jhd->hij', q_heads, k_heads) + bias_full
        row_max = lax.optimization_barrier(jnp.max(scores, axis=-1, keepdims=True))
        expo = jnp.exp(scores - row_max)
        denominator = lax.optimization_barrier(jnp.sum(expo, axis=-1))
        weights = lax.optimization_barrier(expo.astype(jnp.bfloat16)).astype(jnp.float32)
        attention_mixture = jnp.einsum('hij,jhd->ihd', weights, v_heads) / jnp.transpose(denominator)[:, :, None]
        modulated_mixture = (attention_mixture.reshape(AMINO_SPAN, FEATURE_DEPTH) * sigmoid_factors).astype(jnp.bfloat16)
        return jnp.dot(modulated_mixture, final_projection_matrix, preferred_element_type=jnp.float32).astype(jnp.bfloat16)
    return lax.map(attend_row, standardized_alignment)
```

```python
import functools

import jax
import jax.numpy as jnp
from jax import lax
from jax.experimental import pallas as pl
from jax.experimental.pallas import tpu as pltpu
from jax.sharding import PartitionSpec as P

MESH = pl.DeviceIdType.MESH
BF16, F32 = jnp.bfloat16, jnp.float32
SEQS, ROWS, WIDTH, HEADS, HEAD = 4, 128, 256, 8, 32
PAIRS, BLOCK = HEADS // 2, 2 * ROWS
NX, NY, NZL, NZH = 4, 8, 2, 4
AUG = 80
NEG = -1e30


def dot(a, b):
    return jnp.dot(a, b, preferred_element_type=F32)


def dot_nt(a, b):
    return lax.dot_general(a, b, (((1,), (1,)), ((), ())), preferred_element_type=F32)


def normalise(rows, gain):
    wide = rows.astype(F32)
    center = jnp.mean(wide, axis=-1, keepdims=True)
    moved = wide - center
    variance = jnp.mean(moved * moved, axis=-1, keepdims=True)
    return (moved * lax.rsqrt(variance + 1e-05) * gain).astype(BF16)


def query_side(xn, wq, wg, qz, gt):
    wqt, wgt = wq[...].T, wg[...].T
    qz[...] = jnp.zeros_like(qz)
    for s in range(SEQS):
        rows = xn(s)
        qt = (dot_nt(wqt, rows) * HEAD**-0.5).astype(BF16)
        for h in range(HEADS):
            p, half = h // 2, h % 2
            qz[s, p, h * HEAD : (h + 1) * HEAD, half * ROWS : (half + 1) * ROWS] = qt[
                h * HEAD : (h + 1) * HEAD
            ]
        gt[s] = jax.nn.sigmoid(dot_nt(wgt, rows))


def key_side(xg, zh, core, c, slot, wk, wvt, kbuf, vt):
    wvt_all = wvt[...]
    for s in range(SEQS):
        rows = xg[zh, core, s]
        kbuf[slot, s, c * ROWS : (c + 1) * ROWS, :] = dot(rows, wk[...]).astype(BF16)
        values = dot_nt(wvt_all, rows).astype(BF16)
        for p in range(PAIRS):
            vt[slot, s, p, : 2 * HEAD, c * ROWS : (c + 1) * ROWS] = values[
                2 * HEAD * p : 2 * HEAD * (p + 1)
            ]


def bias_block(bta, btb, h, zl, ys):
    pieces = []
    for y in ys:
        for x in range(NX):
            if h < HEADS // 2:
                pieces.append(bta[y, zl, x, h])
            else:
                pieces.append(btb[x, zl, y, h - HEADS // 2])
    return jnp.concatenate(pieces, axis=0).astype(F32)


def attend(slot, zh, core, first, pairs, kbuf, vt, qz, bta, btb, m_ref, l_ref, acc):
    zl = zh // (NZH // NZL)
    y0 = lax.rem(zh, NZH // NZL) * (NY // 2)
    ys = [y0 + 2 * core, y0 + 2 * core + 1, y0 + 2 * (1 - core), y0 + 2 * (1 - core) + 1]

    def body(s, carry):
        keys = kbuf[slot, s]
        for p in pairs:
            scores = dot(keys, qz[s, p])
            scores = scores + jnp.concatenate(
                [bias_block(bta, btb, 2 * p + i, zl, ys) for i in range(2)], axis=1
            )
            top = jnp.max(scores, axis=0, keepdims=True)
            if not first:
                old = m_ref[s, p]
                top = jnp.maximum(old, top)
            weights = jnp.exp(scores - top).astype(BF16)
            mixed = dot(vt[slot, s, p], weights)
            total = mixed[2 * HEAD : 2 * HEAD + 1]
            left, right = mixed[:HEAD, :ROWS], mixed[HEAD : 2 * HEAD, ROWS:]
            if not first:
                scale = jnp.exp(old - top)
                total = l_ref[s, p] * scale + total
                left = acc[s, p, 0] * scale[:, :ROWS] + left
                right = acc[s, p, 1] * scale[:, ROWS:] + right
            m_ref[s, p] = top
            l_ref[s, p] = total
            acc[s, p, 0] = left
            acc[s, p, 1] = right
        return carry

    lax.fori_loop(0, SEQS, body, 0)


def finish(wo, gt, l_ref, acc, out):
    for s in range(SEQS):
        parts = []
        for p in range(PAIRS):
            for half in range(2):
                h = 2 * p + half
                total = l_ref[s, p, :, half * ROWS : (half + 1) * ROWS]
                parts.append(acc[s, p, half] / total * gt[s, h * HEAD : (h + 1) * HEAD])
        gated = jnp.concatenate(parts, axis=0).astype(BF16)
        out[s] = dot(gated.T, wo[...]).astype(BF16)


def kernel(
    x_hbm, gain_hbm, wq_hbm, wk_hbm, wv_hbm, wg_hbm, wo_hbm, b_hbm, out,
    x, gain, wq, wk, wv, wg, wo, b,
    xg, bta, btb, wvt, kbuf, vt, qz, gt, m_ref, l_ref, acc,
    local, xs, xr, as_, ar, bs, br,
):
    seq, res = lax.axis_index("seq"), lax.axis_index("res")
    zl, y, xx = seq // (NY * NX), lax.rem(seq // NX, NY), lax.rem(seq, NX)
    zh, core = res // 2, lax.rem(res, 2)

    def at_seq(zl_, y_, x_):
        return (zl_ * (NY * NX) + y_ * NX + x_, res)

    def at_res(zh_, core_):
        return (seq, zh_ * 2 + core_)

    def mod(v, n):
        return lax.rem(v + n, n)

    z_next, z_prev = mod(zh + 1, NZH), mod(zh - 1, NZH)
    y_next, y_prev = mod(y + 1, NY), mod(y - 1, NY)
    x_next, x_prev = mod(xx + 1, NX), mod(xx - 1, NX)
    dev_zn, dev_zp, dev_sib = at_res(z_next, core), at_res(z_prev, core), at_res(zh, 1 - core)
    dev_yn, dev_yp = at_seq(zl, y_next, xx), at_seq(zl, y_prev, xx)
    dev_xn, dev_xp = at_seq(zl, y, x_next), at_seq(zl, y, x_prev)
    dev_zl = at_seq(1 - zl, y, xx)

    barrier = pltpu.get_barrier_semaphore()
    peers = (dev_zn, dev_zp, dev_sib, dev_yn, dev_yp, dev_xn, dev_xp, dev_zl)
    for peer in peers:
        pl.semaphore_signal(barrier, inc=1, device_id=peer, device_id_type=MESH)

    loads = [
        pltpu.make_async_copy(src, dst, local.at[i])
        for i, (src, dst) in enumerate(
            [(x_hbm, x), (gain_hbm, gain), (b_hbm, b), (wk_hbm, wk), (wv_hbm, wv), (wq_hbm, wq), (wg_hbm, wg), (wo_hbm, wo)]
        )
    ]
    for load in loads:
        load.start()
    loads[0].wait()
    loads[1].wait()
    for s in range(SEQS):
        xg[zh, core, s] = normalise(x[s], gain[...])
    loads[2].wait()
    half_heads = HEADS // 2
    bta[y, zl, xx] = b[:half_heads]
    btb[xx, zl, y] = b[half_heads:]

    started = []

    def send(ref, dev, sems, i):
        copy = pltpu.make_async_remote_copy(
            src_ref=ref, dst_ref=ref, send_sem=sems[0].at[i], recv_sem=sems[1].at[i],
            device_id=dev, device_id_type=MESH,
        )
        copy.start()
        started.append(copy)

    def arrive(ref, sems, i):
        pltpu.make_async_remote_copy(
            src_ref=ref, dst_ref=ref, send_sem=sems[0].at[i], recv_sem=sems[1].at[i],
            device_id=dev_sib, device_id_type=MESH,
        ).wait_recv()

    sx, sa, sb = (xs, xr), (as_, ar), (bs, br)
    lo, hi = pl.ds(0, 2), pl.ds(2, 2)

    pl.semaphore_wait(barrier, len(peers))

    send(bta.at[y, zl, xx], dev_zl, sa, 0)
    send(btb.at[xx, zl, y], dev_zl, sb, 0)
    send(xg.at[zh, core, lo], dev_zn, sx, 0)
    send(xg.at[zh, core, hi], dev_zp, sx, 1)
    send(xg.at[zh, core, hi], dev_zn, sx, 2)
    send(xg.at[zh, core, lo], dev_zp, sx, 3)
    send(xg.at[zh, core], dev_sib, sx, 4)

    arrive(bta.at[y, 1 - zl, xx], sa, 0)
    send(bta.at[y, :, xx], dev_xn, sa, 1)
    send(bta.at[y, :, xx], dev_xp, sa, 2)
    arrive(btb.at[xx, 1 - zl, y], sb, 0)
    send(btb.at[xx, :, y], dev_yn, sb, 1)
    send(btb.at[xx, :, y], dev_yp, sb, 2)

    loads[3].wait()
    loads[4].wait()
    wvt[...] = wv[...].T
    ones = jnp.ones((AUG - 2 * HEAD, BLOCK), BF16)
    for slot in range(NZH):
        for s in range(SEQS):
            for p in range(PAIRS):
                vt[slot, s, p, 2 * HEAD :] = ones

    arrive(bta.at[y, :, x_prev], sa, 1)
    send(bta.at[y, 0, x_prev], dev_xn, sa, 3)
    arrive(bta.at[y, :, x_next], sa, 2)
    send(bta.at[y, 1, x_next], dev_xp, sa, 4)
    arrive(btb.at[xx, :, y_prev], sb, 1)
    send(btb.at[xx, :, y_prev], dev_yn, sb, 3)
    arrive(btb.at[xx, :, y_next], sb, 2)
    send(btb.at[xx, :, y_next], dev_yp, sb, 4)

    loads[5].wait()
    loads[6].wait()

    x_opp = mod(xx + 2, NX)
    arrive(bta.at[y, 0, x_opp], sa, 3)
    arrive(bta.at[y, 1, x_opp], sa, 4)
    send(bta.at[y], dev_yn, sa, 5)
    send(bta.at[y], dev_yp, sa, 6)
    query_side(lambda s: xg[zh, core, s], wq, wg, qz, gt)

    y_prev2, y_next2 = mod(y - 2, NY), mod(y + 2, NY)
    y_prev3, y_next3 = mod(y - 3, NY), mod(y + 3, NY)
    y_opp = mod(y + 4, NY)
    arrive(btb.at[xx, :, y_prev2], sb, 3)
    send(btb.at[xx, :, y_prev2], dev_yn, sb, 5)
    arrive(btb.at[xx, :, y_next2], sb, 4)
    send(btb.at[xx, :, y_next2], dev_yp, sb, 6)
    key_side(xg, zh, core, 0, 0, wk, wvt, kbuf, vt)
    arrive(btb.at[xx, :, y_prev3], sb, 5)
    send(btb.at[xx, 0, y_prev3], dev_yn, sb, 7)
    arrive(btb.at[xx, :, y_next3], sb, 6)
    send(btb.at[xx, 1, y_next3], dev_yp, sb, 8)
    arrive(bta.at[y_prev], sa, 5)
    send(bta.at[y_prev], dev_yn, sa, 7)
    arrive(bta.at[y_next], sa, 6)
    send(bta.at[y_next], dev_yp, sa, 8)
    arrive(btb.at[xx, 0, y_opp], sb, 7)
    arrive(btb.at[xx, 1, y_opp], sb, 8)
    send(btb.at[xx], dev_xn, sb, 9)
    send(btb.at[xx], dev_xp, sb, 10)

    arrive(xg.at[z_prev, core, lo], sx, 0)
    send(xg.at[z_prev, core, lo], dev_zn, sx, 5)
    send(xg.at[z_prev, core, lo], dev_sib, sx, 7)
    arrive(xg.at[z_next, core, hi], sx, 1)
    send(xg.at[z_next, core, hi], dev_zp, sx, 6)
    send(xg.at[z_next, core, hi], dev_sib, sx, 8)
    arrive(bta.at[y_prev2], sa, 7)
    send(bta.at[y_prev2], dev_yn, sa, 9)
    arrive(bta.at[y_next2], sa, 8)
    send(bta.at[y_next2], dev_yp, sa, 10)
    arrive(xg.at[zh, 1 - core], sx, 4)
    key_side(xg, zh, 1 - core, 1, 0, wk, wvt, kbuf, vt)
    arrive(bta.at[y_prev3], sa, 9)
    send(bta.at[y_prev3, 0], dev_yn, sa, 11)
    arrive(bta.at[y_next3], sa, 10)
    send(bta.at[y_next3, 1], dev_yp, sa, 12)
    arrive(btb.at[x_prev], sb, 9)
    send(btb.at[x_prev, 0], dev_xn, sb, 11)
    arrive(btb.at[x_next], sb, 10)
    send(btb.at[x_next, 1], dev_xp, sb, 12)

    arrive(xg.at[z_prev, core, hi], sx, 2)
    send(xg.at[z_prev, core, hi], dev_sib, sx, 9)
    arrive(xg.at[z_next, core, lo], sx, 3)
    send(xg.at[z_next, core, lo], dev_sib, sx, 10)
    key_side(xg, z_prev, core, 0, 1, wk, wvt, kbuf, vt)
    key_side(xg, z_next, core, 0, 2, wk, wvt, kbuf, vt)
    arrive(xg.at[z_prev, 1 - core, lo], sx, 7)
    arrive(xg.at[z_prev, 1 - core, hi], sx, 9)
    key_side(xg, z_prev, 1 - core, 1, 1, wk, wvt, kbuf, vt)
    arrive(xg.at[z_next, 1 - core, hi], sx, 8)
    arrive(xg.at[z_next, 1 - core, lo], sx, 10)
    key_side(xg, z_next, 1 - core, 1, 2, wk, wvt, kbuf, vt)

    arrive(bta.at[y_opp, 0], sa, 11)
    arrive(bta.at[y_opp, 1], sa, 12)
    arrive(btb.at[x_opp, 0], sb, 11)
    arrive(btb.at[x_opp, 1], sb, 12)
    state = (kbuf, vt, qz, bta, btb, m_ref, l_ref, acc)
    pairs = range(PAIRS)
    attend(0, zh, core, True, pairs, *state)
    z_opp = mod(zh + 2, NZH)
    arrive(xg.at[z_opp, core, lo], sx, 5)
    send(xg.at[z_opp, core, lo], dev_sib, sx, 11)
    arrive(xg.at[z_opp, core, hi], sx, 6)
    send(xg.at[z_opp, core, hi], dev_sib, sx, 12)
    attend(1, z_prev, core, False, pairs, *state)
    attend(2, z_next, core, False, pairs, *state)
    key_side(xg, z_opp, core, 0, 3, wk, wvt, kbuf, vt)
    arrive(xg.at[z_opp, 1 - core, lo], sx, 11)
    arrive(xg.at[z_opp, 1 - core, hi], sx, 12)
    key_side(xg, z_opp, 1 - core, 1, 3, wk, wvt, kbuf, vt)
    attend(3, z_opp, core, False, pairs, *state)
    loads[7].wait()
    finish(wo, gt, l_ref, acc, out)
    for copy in started:
        copy.wait_send()


def scratch():
    sem = pltpu.SemaphoreType.DMA
    mat = pltpu.VMEM((WIDTH, WIDTH), BF16)
    half = HEADS // 2
    return [
        pltpu.VMEM((SEQS, ROWS, WIDTH), BF16),
        pltpu.VMEM((1, WIDTH), F32),
        mat, mat, mat, mat, mat,
        pltpu.VMEM((HEADS, 16, ROWS), BF16),
        pltpu.VMEM((NZH, 2, SEQS, ROWS, WIDTH), BF16),
        pltpu.VMEM((NY, NZL, NX, half, 16, ROWS), BF16),
        pltpu.VMEM((NX, NZL, NY, half, 16, ROWS), BF16),
        mat,
        pltpu.VMEM((NZH, SEQS, BLOCK, WIDTH), BF16),
        pltpu.VMEM((NZH, SEQS, PAIRS, AUG, BLOCK), BF16),
        pltpu.VMEM((SEQS, PAIRS, WIDTH, BLOCK), BF16),
        pltpu.VMEM((SEQS, WIDTH, ROWS), F32),
        pltpu.VMEM((SEQS, PAIRS, 1, BLOCK), F32),
        pltpu.VMEM((SEQS, PAIRS, 1, BLOCK), F32),
        pltpu.VMEM((SEQS, PAIRS, 2, HEAD, ROWS), F32),
        sem((8,)),
        sem((13,)), sem((13,)), sem((13,)), sem((13,)), sem((13,)), sem((13,)),
    ]


def on_device(x, gain, wq, wk, wv, wg, wo, b):
    any_space = pl.BlockSpec(memory_space=pltpu.HBM)
    return pl.pallas_call(
        kernel,
        out_shape=jax.ShapeDtypeStruct(x.shape, x.dtype),
        in_specs=[any_space] * 8,
        out_specs=pl.BlockSpec(memory_space=pltpu.VMEM),
        scratch_shapes=scratch(),
        compiler_params=pltpu.CompilerParams(
            collective_id=0, has_side_effects=True, vmem_limit_bytes=48 * 1024 * 1024
        ),
        cost_estimate=pl.CostEstimate(flops=6 * 10**9, bytes_accessed=2 * 10**6, transcendentals=5 * 10**6),
    )(x, gain.reshape(1, -1), wq, wk, wv, wg, wo, jnp.swapaxes(b, 1, 2))


def solution(mesh):
    return jax.shard_map(
        on_device,
        mesh=mesh,
        in_specs=(P("seq", "res", None), P(), P(), P(), P(), P(), P(), P(None, "res", "seq")),
        out_specs=P("seq", "res", None),
        check_vma=False,
    )
```

```python
import functools

import jax
import jax.numpy as jnp
from jax import lax
from jax.experimental import pallas as pl
from jax.experimental.pallas import tpu as pltpu
from jax.sharding import PartitionSpec as P

MESH = pl.DeviceIdType.MESH
BF16, F32 = jnp.bfloat16, jnp.float32
SEQS, ROWS, WIDTH, HEADS, HEAD = 4, 128, 256, 8, 32
PAIRS, BLOCK = HEADS // 2, 2 * ROWS
NX, NY, NZL, NZH = 4, 8, 2, 4
AUG = 80
NEG = -1e30


def dot(a, b):
    return jnp.dot(a, b, preferred_element_type=F32)


def dot_nt(a, b):
    return lax.dot_general(a, b, (((1,), (1,)), ((), ())), preferred_element_type=F32)


def normalise(rows, gain):
    wide = rows.astype(F32)
    center = jnp.mean(wide, axis=-1, keepdims=True)
    moved = wide - center
    variance = jnp.mean(moved * moved, axis=-1, keepdims=True)
    return (moved * lax.rsqrt(variance + 1e-05) * gain).astype(BF16)


def query_side(xn, wq, wg, qz, gt):
    wqt, wgt = wq[...].T, wg[...].T
    qz[...] = jnp.zeros_like(qz)
    for s in range(SEQS):
        rows = xn(s)
        qt = (dot_nt(wqt, rows) * HEAD**-0.5).astype(BF16)
        for h in range(HEADS):
            p, half = h // 2, h % 2
            qz[s, p, h * HEAD : (h + 1) * HEAD, half * ROWS : (half + 1) * ROWS] = qt[
                h * HEAD : (h + 1) * HEAD
            ]
        gt[s] = jax.nn.sigmoid(dot_nt(wgt, rows))


def key_side(xg, zh, core, c, slot, wk, wvt, kbuf, vt):
    wvt_all = wvt[...]
    for s in range(SEQS):
        rows = xg[zh, core, s]
        kbuf[slot, s, c * ROWS : (c + 1) * ROWS, :] = dot(rows, wk[...]).astype(BF16)
        values = dot_nt(wvt_all, rows).astype(BF16)
        for p in range(PAIRS):
            vt[slot, s, p, : 2 * HEAD, c * ROWS : (c + 1) * ROWS] = values[
                2 * HEAD * p : 2 * HEAD * (p + 1)
            ]


def bias_block(bta, btb, h, zl, ys):
    pieces = []
    for y in ys:
        for x in range(NX):
            if h < HEADS // 2:
                pieces.append(bta[y, zl, x, h])
            else:
                pieces.append(btb[x, zl, y, h - HEADS // 2])
    return jnp.concatenate(pieces, axis=0).astype(F32)


def attend(slot, zh, core, first, pairs, kbuf, vt, qz, bta, btb, m_ref, l_ref, acc):
    zl = zh // (NZH // NZL)
    y0 = lax.rem(zh, NZH // NZL) * (NY // 2)
    ys = [y0 + 2 * core, y0 + 2 * core + 1, y0 + 2 * (1 - core), y0 + 2 * (1 - core) + 1]

    def bias(p):
        return jnp.concatenate([bias_block(bta, btb, 2 * p + i, zl, ys) for i in range(2)], axis=1)

    def run(items):
        n = len(items)
        old, sc, w = [None] * n, [None] * n, [None] * n

        def one(i):
            s, p = items[i]
            old[i] = None if first else (m_ref[s, p], l_ref[s, p], acc[s, p, 0], acc[s, p, 1])
            sc[i] = dot(kbuf[slot, s], qz[s, p])

        def two(i):
            s, p = items[i]
            scores = sc[i] + bias(p)
            top = jnp.max(scores, axis=0, keepdims=True)
            if not first:
                top = jnp.maximum(old[i][0], top)
            w[i] = (top, jnp.exp(scores - top).astype(BF16))

        def three(i):
            s, p = items[i]
            top, weights = w[i]
            mixed = dot(vt[slot, s, p], weights)
            total = mixed[2 * HEAD : 2 * HEAD + 1]
            left, right = mixed[:HEAD, :ROWS], mixed[HEAD : 2 * HEAD, ROWS:]
            if not first:
                scale = jnp.exp(old[i][0] - top)
                total = old[i][1] * scale + total
                left = old[i][2] * scale[:, :ROWS] + left
                right = old[i][3] * scale[:, ROWS:] + right
            m_ref[s, p], l_ref[s, p], acc[s, p, 0], acc[s, p, 1] = top, total, left, right

        for t in range(n + 4):
            if t < n:
                one(t)
            if 0 <= t - 2 < n:
                two(t - 2)
            if 0 <= t - 4 < n:
                three(t - 4)

    run([(s, p) for s in range(SEQS) for p in pairs])


def finish(wo, gt, l_ref, acc, out):
    for s in range(SEQS):
        parts = []
        for p in range(PAIRS):
            for half in range(2):
                h = 2 * p + half
                total = l_ref[s, p, :, half * ROWS : (half + 1) * ROWS]
                parts.append(acc[s, p, half] / total * gt[s, h * HEAD : (h + 1) * HEAD])
        gated = jnp.concatenate(parts, axis=0).astype(BF16)
        out[s] = dot(gated.T, wo[...]).astype(BF16)


def kernel(
    x_hbm, gain_hbm, wq_hbm, wk_hbm, wv_hbm, wg_hbm, wo_hbm, b_hbm, out,
    x, gain, wq, wk, wv, wg, wo, b,
    xg, bta, btb, wvt, kbuf, vt, qz, gt, m_ref, l_ref, acc,
    local, ready, xs, xr, as_, ar, bs, br,
):
    seq, res = lax.axis_index("seq"), lax.axis_index("res")
    zl, y, xx = seq // (NY * NX), lax.rem(seq // NX, NY), lax.rem(seq, NX)
    zh, core = res // 2, lax.rem(res, 2)

    def at_seq(zl_, y_, x_):
        return (zl_ * (NY * NX) + y_ * NX + x_, res)

    def at_res(zh_, core_):
        return (seq, zh_ * 2 + core_)

    def mod(v, n):
        return lax.rem(v + n, n)

    z_next, z_prev = mod(zh + 1, NZH), mod(zh - 1, NZH)
    y_next, y_prev = mod(y + 1, NY), mod(y - 1, NY)
    x_next, x_prev = mod(xx + 1, NX), mod(xx - 1, NX)
    dev_zn, dev_zp, dev_sib = at_res(z_next, core), at_res(z_prev, core), at_res(zh, 1 - core)
    dev_yn, dev_yp = at_seq(zl, y_next, xx), at_seq(zl, y_prev, xx)
    dev_xn, dev_xp = at_seq(zl, y, x_next), at_seq(zl, y, x_prev)
    dev_zl = at_seq(1 - zl, y, xx)

    barrier = pltpu.get_barrier_semaphore()
    partners = {
        "zn": (dev_zn, zh < z_next, 1), "zp": (dev_zp, zh < z_prev, 0), "sib": (dev_sib, core < 1, 2),
        "yn": (dev_yn, y < y_next, 4), "yp": (dev_yp, y < y_prev, 3), "xn": (dev_xn, xx < x_next, 6), "xp": (dev_xp, xx < x_prev, 5),
        "zl": (dev_zl, zl < 1, 7),
    }
    slots = {name: i for i, name in enumerate(partners)}
    late = 0
    for dev, early, _ in partners.values():
        late = late + jnp.where(early, 0, 1)

        @pl.when(early)
        def _(dev=dev):
            pl.semaphore_signal(barrier, inc=1, device_id=dev, device_id_type=MESH)

    loads = [
        pltpu.make_async_copy(src, dst, local.at[i])
        for i, (src, dst) in enumerate(
            [(x_hbm, x), (gain_hbm, gain), (b_hbm, b), (wk_hbm, wk), (wv_hbm, wv), (wq_hbm, wq), (wg_hbm, wg), (wo_hbm, wo)]
        )
    ]
    for load in loads:
        load.start()
    loads[0].wait()
    loads[1].wait()
    for s in range(SEQS):
        xg[zh, core, s] = normalise(x[s], gain[...])
    loads[2].wait()
    half_heads = HEADS // 2
    bta[y, zl, xx] = b[:half_heads]
    btb[xx, zl, y] = b[half_heads:]

    started = []

    greeted = set()

    def send(ref, name, sems, i):
        dev, early, _ = partners[name]
        if name not in greeted:
            greeted.add(name)

            @pl.when(early)
            def _():
                pl.semaphore_wait(ready.at[slots[name]], 1)

        copy = pltpu.make_async_remote_copy(
            src_ref=ref, dst_ref=ref, send_sem=sems[0].at[i], recv_sem=sems[1].at[i],
            device_id=dev, device_id_type=MESH,
        )
        copy.start()
        started.append(copy)

    def arrive(ref, sems, i):
        pltpu.make_async_remote_copy(
            src_ref=ref, dst_ref=ref, send_sem=sems[0].at[i], recv_sem=sems[1].at[i],
            device_id=dev_sib, device_id_type=MESH,
        ).wait_recv()

    sx, sa, sb = (xs, xr), (as_, ar), (bs, br)
    lo, hi = pl.ds(0, 2), pl.ds(2, 2)

    @pl.when(late > 0)
    def _():
        pl.semaphore_wait(barrier, late)

    for dev, early, slot in partners.values():

        @pl.when(jnp.logical_not(early))
        def _(dev=dev, slot=slot):
            pl.semaphore_signal(ready.at[slot], inc=1, device_id=dev, device_id_type=MESH)

    send(bta.at[y, zl, xx], "zl", sa, 0)
    send(btb.at[xx, zl, y], "zl", sb, 0)
    send(xg.at[zh, core, lo], "zn", sx, 0)
    send(xg.at[zh, core, hi], "zp", sx, 1)
    send(xg.at[zh, core, hi], "zn", sx, 2)
    send(xg.at[zh, core, lo], "zp", sx, 3)
    send(xg.at[zh, core], "sib", sx, 4)

    arrive(bta.at[y, 1 - zl, xx], sa, 0)
    send(bta.at[y, :, xx], "xn", sa, 1)
    send(bta.at[y, :, xx], "xp", sa, 2)
    arrive(btb.at[xx, 1 - zl, y], sb, 0)
    send(btb.at[xx, :, y], "yn", sb, 1)
    send(btb.at[xx, :, y], "yp", sb, 2)

    loads[3].wait()
    loads[4].wait()
    wvt[...] = wv[...].T
    ones = jnp.ones((AUG - 2 * HEAD, BLOCK), BF16)
    for slot in range(NZH):
        for s in range(SEQS):
            for p in range(PAIRS):
                vt[slot, s, p, 2 * HEAD :] = ones

    arrive(bta.at[y, :, x_prev], sa, 1)
    send(bta.at[y, 0, x_prev], "xn", sa, 3)
    arrive(bta.at[y, :, x_next], sa, 2)
    send(bta.at[y, 1, x_next], "xp", sa, 4)
    arrive(btb.at[xx, :, y_prev], sb, 1)
    send(btb.at[xx, :, y_prev], "yn", sb, 3)
    arrive(btb.at[xx, :, y_next], sb, 2)
    send(btb.at[xx, :, y_next], "yp", sb, 4)

    loads[5].wait()
    loads[6].wait()

    x_opp = mod(xx + 2, NX)
    arrive(bta.at[y, 0, x_opp], sa, 3)
    arrive(bta.at[y, 1, x_opp], sa, 4)
    send(bta.at[y], "yn", sa, 5)
    send(bta.at[y], "yp", sa, 6)
    query_side(lambda s: xg[zh, core, s], wq, wg, qz, gt)

    y_prev2, y_next2 = mod(y - 2, NY), mod(y + 2, NY)
    y_prev3, y_next3 = mod(y - 3, NY), mod(y + 3, NY)
    y_opp = mod(y + 4, NY)
    arrive(btb.at[xx, :, y_prev2], sb, 3)
    send(btb.at[xx, :, y_prev2], "yn", sb, 5)
    arrive(btb.at[xx, :, y_next2], sb, 4)
    send(btb.at[xx, :, y_next2], "yp", sb, 6)
    key_side(xg, zh, core, 0, 0, wk, wvt, kbuf, vt)
    arrive(btb.at[xx, :, y_prev3], sb, 5)
    send(btb.at[xx, 0, y_prev3], "yn", sb, 7)
    arrive(btb.at[xx, :, y_next3], sb, 6)
    send(btb.at[xx, 1, y_next3], "yp", sb, 8)
    arrive(bta.at[y_prev], sa, 5)
    send(bta.at[y_prev], "yn", sa, 7)
    arrive(bta.at[y_next], sa, 6)
    send(bta.at[y_next], "yp", sa, 8)
    arrive(btb.at[xx, 0, y_opp], sb, 7)
    arrive(btb.at[xx, 1, y_opp], sb, 8)
    send(btb.at[xx], "xn", sb, 9)
    send(btb.at[xx], "xp", sb, 10)

    arrive(xg.at[z_prev, core, lo], sx, 0)
    send(xg.at[z_prev, core, lo], "zn", sx, 5)
    send(xg.at[z_prev, core, lo], "sib", sx, 7)
    arrive(xg.at[z_next, core, hi], sx, 1)
    send(xg.at[z_next, core, hi], "zp", sx, 6)
    send(xg.at[z_next, core, hi], "sib", sx, 8)
    arrive(bta.at[y_prev2], sa, 7)
    send(bta.at[y_prev2], "yn", sa, 9)
    arrive(bta.at[y_next2], sa, 8)
    send(bta.at[y_next2], "yp", sa, 10)
    arrive(xg.at[zh, 1 - core], sx, 4)
    key_side(xg, zh, 1 - core, 1, 0, wk, wvt, kbuf, vt)
    arrive(bta.at[y_prev3], sa, 9)
    send(bta.at[y_prev3, 0], "yn", sa, 11)
    arrive(bta.at[y_next3], sa, 10)
    send(bta.at[y_next3, 1], "yp", sa, 12)
    arrive(btb.at[x_prev], sb, 9)
    send(btb.at[x_prev, 0], "xn", sb, 11)
    arrive(btb.at[x_next], sb, 10)
    send(btb.at[x_next, 1], "xp", sb, 12)

    arrive(xg.at[z_prev, core, hi], sx, 2)
    send(xg.at[z_prev, core, hi], "sib", sx, 9)
    arrive(xg.at[z_next, core, lo], sx, 3)
    send(xg.at[z_next, core, lo], "sib", sx, 10)
    key_side(xg, z_prev, core, 0, 1, wk, wvt, kbuf, vt)
    key_side(xg, z_next, core, 0, 2, wk, wvt, kbuf, vt)
    arrive(xg.at[z_prev, 1 - core, lo], sx, 7)
    arrive(xg.at[z_prev, 1 - core, hi], sx, 9)
    key_side(xg, z_prev, 1 - core, 1, 1, wk, wvt, kbuf, vt)
    arrive(xg.at[z_next, 1 - core, hi], sx, 8)
    arrive(xg.at[z_next, 1 - core, lo], sx, 10)
    key_side(xg, z_next, 1 - core, 1, 2, wk, wvt, kbuf, vt)

    arrive(bta.at[y_opp, 0], sa, 11)
    arrive(bta.at[y_opp, 1], sa, 12)
    arrive(btb.at[x_opp, 0], sb, 11)
    arrive(btb.at[x_opp, 1], sb, 12)
    state = (kbuf, vt, qz, bta, btb, m_ref, l_ref, acc)
    pairs = range(PAIRS)
    attend(0, zh, core, True, pairs, *state)
    z_opp = mod(zh + 2, NZH)
    arrive(xg.at[z_opp, core, lo], sx, 5)
    send(xg.at[z_opp, core, lo], "sib", sx, 11)
    arrive(xg.at[z_opp, core, hi], sx, 6)
    send(xg.at[z_opp, core, hi], "sib", sx, 12)
    attend(1, z_prev, core, False, pairs, *state)
    attend(2, z_next, core, False, pairs, *state)
    key_side(xg, z_opp, core, 0, 3, wk, wvt, kbuf, vt)
    arrive(xg.at[z_opp, 1 - core, lo], sx, 11)
    arrive(xg.at[z_opp, 1 - core, hi], sx, 12)
    key_side(xg, z_opp, 1 - core, 1, 3, wk, wvt, kbuf, vt)
    attend(3, z_opp, core, False, pairs, *state)
    loads[7].wait()
    finish(wo, gt, l_ref, acc, out)
    for copy in started:
        copy.wait_send()


def scratch():
    sem = pltpu.SemaphoreType.DMA
    mat = pltpu.VMEM((WIDTH, WIDTH), BF16)
    half = HEADS // 2
    return [
        pltpu.VMEM((SEQS, ROWS, WIDTH), BF16),
        pltpu.VMEM((1, WIDTH), F32),
        mat, mat, mat, mat, mat,
        pltpu.VMEM((HEADS, 16, ROWS), BF16),
        pltpu.VMEM((NZH, 2, SEQS, ROWS, WIDTH), BF16),
        pltpu.VMEM((NY, NZL, NX, half, 16, ROWS), BF16),
        pltpu.VMEM((NX, NZL, NY, half, 16, ROWS), BF16),
        mat,
        pltpu.VMEM((NZH, SEQS, BLOCK, WIDTH), BF16),
        pltpu.VMEM((NZH, SEQS, PAIRS, AUG, BLOCK), BF16),
        pltpu.VMEM((SEQS, PAIRS, WIDTH, BLOCK), BF16),
        pltpu.VMEM((SEQS, WIDTH, ROWS), F32),
        pltpu.VMEM((SEQS, PAIRS, 1, BLOCK), F32),
        pltpu.VMEM((SEQS, PAIRS, 1, BLOCK), F32),
        pltpu.VMEM((SEQS, PAIRS, 2, HEAD, ROWS), F32),
        sem((8,)), pltpu.SemaphoreType.REGULAR((8,)),
        sem((13,)), sem((13,)), sem((13,)), sem((13,)), sem((13,)), sem((13,)),
    ]


def on_device(x, gain, wq, wk, wv, wg, wo, b):
    any_space = pl.BlockSpec(memory_space=pltpu.HBM)
    return pl.pallas_call(
        kernel,
        out_shape=jax.ShapeDtypeStruct(x.shape, x.dtype),
        in_specs=[any_space] * 8,
        out_specs=pl.BlockSpec(memory_space=pltpu.VMEM),
        scratch_shapes=scratch(),
        compiler_params=pltpu.CompilerParams(
            collective_id=0, has_side_effects=True, vmem_limit_bytes=63 * 1024 * 1024
        ),
        cost_estimate=pl.CostEstimate(flops=6 * 10**9, bytes_accessed=2 * 10**6, transcendentals=5 * 10**6),
    )(x, gain.reshape(1, -1), wq, wk, wv, wg, wo, jnp.swapaxes(b, 1, 2))


def solution(mesh):
    return jax.shard_map(
        on_device,
        mesh=mesh,
        in_specs=(P("seq", "res", None), P(), P(), P(), P(), P(), P(), P(None, "res", "seq")),
        out_specs=P("seq", "res", None),
        check_vma=False,
    )
```

```python
import functools

import jax
import jax.numpy as jnp
from jax import lax
from jax.experimental import pallas as pl
from jax.experimental.pallas import tpu as pltpu
from jax.sharding import PartitionSpec as P

MESH = pl.DeviceIdType.MESH
BF16, F32 = jnp.bfloat16, jnp.float32
SEQS, ROWS, WIDTH, HEADS, HEAD = 4, 128, 256, 8, 32
PAIRS, BLOCK = HEADS // 2, 2 * ROWS
NX, NY, NZL, NZH = 4, 8, 2, 4
AUG = 80
FIRST = 3
COPIES = 80
TA, TB, TX, EN, EP = 4.0, 1.5, (7.5, 10.0), 2.2, 5.0
TL = {"zn": (7.5, 10.0), "zp": (7.5, 10.0)}


def dot(a, b):
    return jnp.dot(a, b, preferred_element_type=F32)


def dot_nt(a, b):
    return lax.dot_general(a, b, (((1,), (1,)), ((), ())), preferred_element_type=F32)


def normalise(rows, gain):
    wide = rows.astype(F32)
    center = jnp.mean(wide, axis=-1, keepdims=True)
    moved = wide - center
    variance = jnp.mean(moved * moved, axis=-1, keepdims=True)
    return (moved * lax.rsqrt(variance + 1e-05) * gain).astype(BF16)


def query_side(xn, wq, wg, qz, gt):
    wqt, wgt = wq[...].T, wg[...].T
    qz[...] = jnp.zeros_like(qz)
    for s in range(SEQS):
        rows = xn(s)
        qt = (dot_nt(wqt, rows) * HEAD**-0.5).astype(BF16)
        for h in range(HEADS):
            p, half = h // 2, h % 2
            qz[s, p, h * HEAD : (h + 1) * HEAD, half * ROWS : (half + 1) * ROWS] = qt[
                h * HEAD : (h + 1) * HEAD
            ]
        gt[s] = jax.nn.sigmoid(dot_nt(wgt, rows))


def key_side(xg, zh, core, c, slot, wk, wvt, kbuf, vt):
    wvt_all = wvt[...]
    for s in range(SEQS):
        rows = xg[zh, core, s]
        kbuf[slot, s, c * ROWS : (c + 1) * ROWS, :] = dot(rows, wk[...]).astype(BF16)
        values = dot_nt(wvt_all, rows).astype(BF16)
        for p in range(PAIRS):
            vt[slot, s, p, : 2 * HEAD, c * ROWS : (c + 1) * ROWS] = values[
                2 * HEAD * p : 2 * HEAD * (p + 1)
            ]


def bias_block(bta, btb, h, zl, ys):
    pieces = []
    for y in ys:
        for x in range(NX):
            if h < FIRST:
                pieces.append(bta[y, zl, x, h])
            else:
                pieces.append(btb[x, zl, y, h - FIRST])
    return jnp.concatenate(pieces, axis=0).astype(F32)


def attend(slot, zh, core, first, pairs, kbuf, vt, qz, bta, btb, m_ref, l_ref, acc):
    zl = zh // (NZH // NZL)
    y0 = lax.rem(zh, NZH // NZL) * (NY // 2)
    ys = [y0 + 2 * core, y0 + 2 * core + 1, y0 + 2 * (1 - core), y0 + 2 * (1 - core) + 1]

    def bias(p):
        return jnp.concatenate([bias_block(bta, btb, 2 * p + i, zl, ys) for i in range(2)], axis=1)

    def run(items):
        n = len(items)
        old, sc, w = [None] * n, [None] * n, [None] * n

        def one(i):
            s, p = items[i]
            old[i] = None if first else (m_ref[s, p], l_ref[s, p], acc[s, p, 0], acc[s, p, 1])
            sc[i] = dot(kbuf[slot, s], qz[s, p])

        def two(i):
            s, p = items[i]
            scores = sc[i] + bias(p)
            top = jnp.max(scores, axis=0, keepdims=True)
            if not first:
                top = jnp.maximum(old[i][0], top)
            w[i] = (top, jnp.exp(scores - top).astype(BF16))

        def three(i):
            s, p = items[i]
            top, weights = w[i]
            mixed = dot(vt[slot, s, p], weights)
            total = mixed[2 * HEAD : 2 * HEAD + 1]
            left, right = mixed[:HEAD, :ROWS], mixed[HEAD : 2 * HEAD, ROWS:]
            if not first:
                scale = jnp.exp(old[i][0] - top)
                total = old[i][1] * scale + total
                left = old[i][2] * scale[:, :ROWS] + left
                right = old[i][3] * scale[:, ROWS:] + right
            m_ref[s, p], l_ref[s, p], acc[s, p, 0], acc[s, p, 1] = top, total, left, right

        for t in range(n + 4):
            if t < n:
                one(t)
            if 0 <= t - 2 < n:
                two(t - 2)
            if 0 <= t - 4 < n:
                three(t - 4)

    run([(s, p) for s in range(SEQS) for p in pairs])


def finish(wo, gt, l_ref, acc, held, out, sems):
    copies = []
    for s in range(SEQS):
        parts = []
        for p in range(PAIRS):
            for half in range(2):
                h = 2 * p + half
                total = l_ref[s, p, :, half * ROWS : (half + 1) * ROWS]
                parts.append(acc[s, p, half] / total * gt[s, h * HEAD : (h + 1) * HEAD])
        gated = jnp.concatenate(parts, axis=0).astype(BF16)
        held[s] = dot(gated.T, wo[...]).astype(BF16)
        copies.append(pltpu.make_async_copy(held.at[s], out.at[s], sems.at[s]))
        copies[-1].start()
    for copy in copies:
        copy.wait()


def kernel(
    x_hbm, gain_hbm, wq_hbm, wk_hbm, wv_hbm, wg_hbm, wo_hbm, b_hbm, out,
    x, gain, wq, wk, wv, wg, wo, b,
    xg, bta, btb, wvt, kbuf, vt, qz, gt, m_ref, l_ref, acc,
    local, ready, sent, received,
):
    seq, res = lax.axis_index("seq"), lax.axis_index("res")
    zl, y, xx = seq // (NY * NX), lax.rem(seq // NX, NY), lax.rem(seq, NX)
    zh, core = res // 2, lax.rem(res, 2)

    def at_seq(zl_, y_, x_):
        return (zl_ * (NY * NX) + y_ * NX + x_, res)

    def at_res(zh_, core_):
        return (seq, zh_ * 2 + core_)

    def mod(v, n):
        return lax.rem(v + n, n)

    def y_at(k):
        return mod(y + k, NY)

    z_next, z_prev, z_opp = mod(zh + 1, NZH), mod(zh - 1, NZH), mod(zh + 2, NZH)
    y_next, y_prev = y_at(1), y_at(-1)
    x_next, x_prev, x_opp = mod(xx + 1, NX), mod(xx - 1, NX), mod(xx + 2, NX)
    z_side = (zl, 1 - zl)

    barrier = pltpu.get_barrier_semaphore()
    partners = {
        "zn": (at_res(z_next, core), zh < z_next, 1),
        "zp": (at_res(z_prev, core), zh < z_prev, 0),
        "sib": (at_res(zh, 1 - core), core < 1, 2),
        "yn": (at_seq(zl, y_next, xx), y < y_next, 4),
        "yp": (at_seq(zl, y_prev, xx), y < y_prev, 3),
        "xn": (at_seq(zl, y, x_next), xx < x_next, 6),
        "xp": (at_seq(zl, y, x_prev), xx < x_prev, 5),
        "xo": (at_seq(zl, y, x_opp), xx < x_opp, 7),
        "zl": (at_seq(1 - zl, y, xx), zl < 1, 8),
    }
    slots = {name: i for i, name in enumerate(partners)}
    late = 0
    for dev, early, _ in partners.values():
        late = late + jnp.where(early, 0, 1)

        @pl.when(early)
        def _(dev=dev):
            pl.semaphore_signal(barrier, inc=1, device_id=dev, device_id_type=MESH)

    loads = [
        pltpu.make_async_copy(src, dst, local.at[i])
        for i, (src, dst) in enumerate(
            [(x_hbm, x), (gain_hbm, gain), (b_hbm, b), (wk_hbm, wk), (wv_hbm, wv), (wq_hbm, wq), (wg_hbm, wg), (wo_hbm, wo)]
        )
    ]
    for load in loads:
        load.start()
    @pl.when(late > 0)
    def _():
        pl.semaphore_wait(barrier, late)

    for dev, early, slot in partners.values():

        @pl.when(jnp.logical_not(early))
        def _(dev=dev, slot=slot):
            pl.semaphore_signal(ready.at[slot], inc=1, device_id=dev, device_id_type=MESH)

    loads[0].wait()
    loads[1].wait()
    for s in range(SEQS):
        xg[zh, core, s] = normalise(x[s], gain[...])
    loads[2].wait()
    bta[y, zl, xx] = b[:FIRST]
    btb[xx, zl, y] = b[FIRST:]

    started, greeted, numbers = [], set(), {}

    def copy_of(key, ref, name):
        i = numbers.setdefault(key, len(numbers))
        return pltpu.make_async_remote_copy(
            src_ref=ref, dst_ref=ref, send_sem=sent.at[i], recv_sem=received.at[i],
            device_id=partners[name][0], device_id_type=MESH,
        )

    def greet(name):
        if name not in greeted:
            greeted.add(name)

            @pl.when(partners[name][1])
            def _():
                pl.semaphore_wait(ready.at[slots[name]], 1)

    def send(key, ref, name):
        greet(name)
        copy = copy_of(key, ref, name)
        copy.start()
        started.append(copy)

    def arrive(key, ref):
        copy_of(key, ref, "sib").wait_recv()

    plan = []

    def at(time):
        def add(step):
            plan.append((time, len(plan), step))
            return step

        return add

    across = (("xn", x_prev), ("xp", x_next), ("xo", x_opp))

    @at(0)
    def _():
        send(("bz",), btb.at[xx, zl, y], "zl")
        send(("az",), bta.at[y, zl, xx], "zl")
        for name, _ in across:
            send(("ax", 0, name), bta.at[y, zl, xx], name)

    @at(1.31)
    def _():
        arrive(("az",), bta.at[y, 1 - zl, xx])
        for name, _ in across:
            send(("ax", 1, name), bta.at[y, 1 - zl, xx], name)

    for half in range(2):

        @at(1.5 + 1.3 * half)
        def _(half=half):
            for name, origin in across:
                arrive(("ax", half, name), bta.at[y, z_side[half], origin])
            for name in ("yn", "yp"):
                send(("ay", 0, half, name), bta.at[y, z_side[half]], name)

        for k in range(1, 4):

            @at(TA + 2.2 * (k - 1) + 1.1 * half)
            def _(k=k, half=half):
                for name, step, far in (("yn", -k, 0), ("yp", k, 1)):
                    slab = bta.at[y_at(step), z_side[half]]
                    arrive(("ay", k - 1, half, name), slab)
                    if k < 3 or half == far:
                        send(("ay", k, half, name), slab, name)

    @at(TA + 7.4)
    def _():
        arrive(("ay", 3, 0, "yn"), bta.at[y_at(4), z_side[0]])
        arrive(("ay", 3, 1, "yp"), bta.at[y_at(4), z_side[1]])

    def spread(k):
        for name in ("xn", "xp"):
            send(("bx", k, name), btb.at[xx, :, y_at(k)], name)

    @at(1.3)
    def _():
        arrive(("bz",), btb.at[xx, 1 - zl, y])
        for name in ("yn", "yp"):
            send(("by", 0, name), btb.at[xx, :, y], name)
        spread(0)

    for k in range(1, 4):

        @at(1.3 + TB * k)
        def _(k=k):
            for name, step, far in (("yn", -k, 0), ("yp", k, 1)):
                slab = btb.at[xx, :, y_at(step)]
                arrive(("by", k - 1, name), slab)
                send(("by", k, name), slab if k < 3 else btb.at[xx, z_side[far], y_at(step)], name)
            spread(-k)
            spread(k)

    @at(1.3 + TB * 4)
    def _():
        arrive(("by", 3, "yn"), btb.at[xx, z_side[0], y_at(4)])
        arrive(("by", 3, "yp"), btb.at[xx, z_side[1], y_at(4)])
        spread(4)

    order = (0, -1, 1, -2, 2, -3, 3, 4)
    for i, k in enumerate(order):

        @at(max(2.9 + 0.85 * i, 1.4 + TB * abs(k) + 1.4))
        def _(i=i, k=k):
            arrive(("bx", k, "xn"), btb.at[x_prev, :, y_at(k)])
            arrive(("bx", k, "xp"), btb.at[x_next, :, y_at(k)])
            if i in (0, 1, 4, 5):
                send(("bo", k), btb.at[x_prev, :, y_at(k)], "xn")
            else:
                send(("bo", k), btb.at[x_next, :, y_at(k)], "xp")

    @at(11.9)
    def _():
        for k in order:
            arrive(("bo", k), btb.at[x_opp, :, y_at(k)])

    halves = (slice(0, SEQS // 2), slice(SEQS // 2, SEQS))
    first_half = {"zn": 0, "zp": 1}

    def rows_to(name, when_early):
        early = partners[name][1]
        greeted.add(name)
        copies = [
            copy_of(("xo", name, i), xg.at[zh, core, halves[first_half[name] ^ i]], name) for i in range(2)
        ]

        @pl.when(early if when_early else jnp.logical_not(early))
        def _():
            if when_early:
                pl.semaphore_wait(ready.at[slots[name]], 1)
            for copy in copies:
                copy.start()

        if when_early:
            started.extend(copies)

    at(0.01)(lambda: rows_to("zp", False))
    at(0.02)(lambda: rows_to("zn", False))
    at(0.03)(lambda: send(("xs",), xg.at[zh, core], "sib"))
    at(EN)(lambda: rows_to("zn", True))
    at(EP)(lambda: rows_to("zp", True))

    def rows_from(name, origin, i):
        part = xg.at[origin, core, halves[first_half[name] ^ i]]
        onward = [copy_of(("xt", name, i), part, "sib")]
        if i == 0:
            onward.append(copy_of(("xf", name), part, name))
        started.extend(onward)
        come = copy_of(("xo", name, i), part, "sib")

        def step():
            come.wait_recv()
            for copy in onward:
                copy.start()

        at(TX[i])(lambda: pl.when(zh >= 2)(step))
        at(TL[name][i])(lambda: pl.when(zh < 2)(step))

    for name, origin in (("zn", z_prev), ("zp", z_next)):
        for i in range(2):
            rows_from(name, origin, i)

    def rows_told(name, origin, i):
        arrive(("xt", name, i), xg.at[origin, 1 - core, halves[first_half[name] ^ i]])

    state = (kbuf, vt, qz, bta, btb, m_ref, l_ref, acc)
    pairs = range(PAIRS)

    @at(0.04)
    def _():
        loads[3].wait()
        loads[4].wait()
        wvt[...] = wv[...].T
        ones = jnp.ones((AUG - 2 * HEAD, BLOCK), BF16)
        for slot in range(NZH):
            for s in range(SEQS):
                for p in range(PAIRS):
                    vt[slot, s, p, 2 * HEAD :] = ones

    @at(1.7)
    def _():
        loads[5].wait()
        loads[6].wait()
        query_side(lambda s: xg[zh, core, s], wq, wg, qz, gt)

    at(3.1)(lambda: key_side(xg, zh, core, 0, 0, wk, wvt, kbuf, vt))

    @at(6.1)
    def _():
        arrive(("xs",), xg.at[zh, 1 - core])
        key_side(xg, zh, 1 - core, 1, 0, wk, wvt, kbuf, vt)

    for slot, (name, origin) in enumerate((("zn", z_prev), ("zp", z_next)), start=1):

        @at(14.1)
        def _(slot=slot, origin=origin):
            key_side(xg, origin, core, 0, slot, wk, wvt, kbuf, vt)

        @at(14.2)
        def _(slot=slot, name=name, origin=origin):
            rows_told(name, origin, 0)
            rows_told(name, origin, 1)
            key_side(xg, origin, 1 - core, 1, slot, wk, wvt, kbuf, vt)

    at(15.0)(lambda: attend(0, zh, core, True, pairs, *state))
    at(15.2)(lambda: attend(1, z_prev, core, False, pairs, *state))

    @at(15.3)
    def _():
        for name in ("zn", "zp"):
            part = xg.at[z_opp, core, halves[first_half[name]]]
            arrive(("xf", name), part)
            send(("xu", name), part, "sib")

    at(15.4)(lambda: attend(2, z_next, core, False, pairs, *state))

    @at(15.5)
    def _():
        key_side(xg, z_opp, core, 0, 3, wk, wvt, kbuf, vt)
        for name in ("zn", "zp"):
            arrive(("xu", name), xg.at[z_opp, 1 - core, halves[first_half[name]]])
        key_side(xg, z_opp, 1 - core, 1, 3, wk, wvt, kbuf, vt)

    at(15.6)(lambda: attend(3, z_opp, core, False, pairs, *state))
    loads_left = loads[7]

    for _, _, step in sorted(plan, key=lambda entry: entry[:2]):
        step()
    loads_left.wait()
    finish(wo, gt, l_ref, acc, x, out, local)
    for copy in started:
        copy.wait_send()


def scratch():
    sem = pltpu.SemaphoreType.DMA
    mat = pltpu.VMEM((WIDTH, WIDTH), BF16)
    return [
        pltpu.VMEM((SEQS, ROWS, WIDTH), BF16),
        pltpu.VMEM((1, WIDTH), F32),
        mat, mat, mat, mat, mat,
        pltpu.VMEM((HEADS, 16, ROWS), BF16),
        pltpu.VMEM((NZH, 2, SEQS, ROWS, WIDTH), BF16),
        pltpu.VMEM((NY, NZL, NX, FIRST, 16, ROWS), BF16),
        pltpu.VMEM((NX, NZL, NY, HEADS - FIRST, 16, ROWS), BF16),
        mat,
        pltpu.VMEM((NZH, SEQS, BLOCK, WIDTH), BF16),
        pltpu.VMEM((NZH, SEQS, PAIRS, AUG, BLOCK), BF16),
        pltpu.VMEM((SEQS, PAIRS, WIDTH, BLOCK), BF16),
        pltpu.VMEM((SEQS, WIDTH, ROWS), F32),
        pltpu.VMEM((SEQS, PAIRS, 1, BLOCK), F32),
        pltpu.VMEM((SEQS, PAIRS, 1, BLOCK), F32),
        pltpu.VMEM((SEQS, PAIRS, 2, HEAD, ROWS), F32),
        sem((8,)), pltpu.SemaphoreType.REGULAR((9,)),
        sem((COPIES,)), sem((COPIES,)),
    ]


def on_device(x, gain, wq, wk, wv, wg, wo, b):
    any_space = pl.BlockSpec(memory_space=pltpu.HBM)
    return pl.pallas_call(
        kernel,
        out_shape=jax.ShapeDtypeStruct(x.shape, x.dtype),
        in_specs=[any_space] * 8,
        out_specs=any_space,
        scratch_shapes=scratch(),
        compiler_params=pltpu.CompilerParams(
            collective_id=0, has_side_effects=True, vmem_limit_bytes=63 * 1024 * 1024
        ),
        cost_estimate=pl.CostEstimate(flops=6 * 10**9, bytes_accessed=2 * 10**6, transcendentals=5 * 10**6),
    )(x, gain.reshape(1, -1), wq, wk, wv, wg, wo, jnp.swapaxes(b, 1, 2))


def solution(mesh):
    return jax.shard_map(
        on_device,
        mesh=mesh,
        in_specs=(P("seq", "res", None), P(), P(), P(), P(), P(), P(), P(None, "res", "seq")),
        out_specs=P("seq", "res", None),
        check_vma=False,
    )
```

```python
import functools

import jax
import jax.numpy as jnp
from jax import lax
from jax.experimental import pallas as pl
from jax.experimental.pallas import tpu as pltpu
from jax.sharding import PartitionSpec as P

MESH = pl.DeviceIdType.MESH
BF16, F32 = jnp.bfloat16, jnp.float32
SEQS, ROWS, WIDTH, HEADS, HEAD = 4, 128, 256, 8, 32
PAIRS, BLOCK = HEADS // 2, 2 * ROWS
NX, NY, NZL, NZH = 4, 8, 2, 4
AUG = 80
FIRST = 3
COPIES = 80
TA, TB, TX, EN, EP = 4.0, 1.5, (7.5, 10.0), 2.2, 5.0
TL = {"zn": (7.5, 10.0), "zp": (7.5, 10.0)}


def dot(a, b):
    return jnp.dot(a, b, preferred_element_type=F32)


def dot_nt(a, b):
    return lax.dot_general(a, b, (((1,), (1,)), ((), ())), preferred_element_type=F32)


def normalise(rows, gain):
    wide = rows.astype(F32)
    center = jnp.mean(wide, axis=-1, keepdims=True)
    moved = wide - center
    variance = jnp.mean(moved * moved, axis=-1, keepdims=True)
    return (moved * lax.rsqrt(variance + 1e-05) * gain).astype(BF16)


def query_side(xn, wq, wg, qz, gt):
    wqt, wgt = wq[...].T, wg[...].T
    qz[...] = jnp.zeros_like(qz)
    for s in range(SEQS):
        rows = xn(s)
        qt = (dot_nt(wqt, rows) * HEAD**-0.5).astype(BF16)
        for h in range(HEADS):
            p, half = h // 2, h % 2
            qz[s, p, h * HEAD : (h + 1) * HEAD, half * ROWS : (half + 1) * ROWS] = qt[
                h * HEAD : (h + 1) * HEAD
            ]
        gt[s] = jax.nn.sigmoid(dot_nt(wgt, rows))


def key_side(xg, zh, core, c, slot, wk, wvt, kbuf, vt):
    wvt_all = wvt[...]
    for s in range(SEQS):
        rows = xg[zh, core, s]
        kbuf[slot, s, c * ROWS : (c + 1) * ROWS, :] = dot(rows, wk[...]).astype(BF16)
        values = dot_nt(wvt_all, rows).astype(BF16)
        for p in range(PAIRS):
            vt[slot, s, p, : 2 * HEAD, c * ROWS : (c + 1) * ROWS] = values[
                2 * HEAD * p : 2 * HEAD * (p + 1)
            ]


def bias_block(bta, btb, h, zl, ys):
    pieces = []
    for y in ys:
        for x in range(NX):
            if h < FIRST:
                pieces.append(bta[y, zl, x, h])
            else:
                pieces.append(btb[x, zl, y, h - FIRST])
    return jnp.concatenate(pieces, axis=0).astype(F32)


def attend(slot, zh, core, first, pairs, kbuf, vt, qz, bta, btb, m_ref, l_ref, acc):
    zl = zh // (NZH // NZL)
    y0 = lax.rem(zh, NZH // NZL) * (NY // 2)
    ys = [y0 + 2 * core, y0 + 2 * core + 1, y0 + 2 * (1 - core), y0 + 2 * (1 - core) + 1]

    def bias(p):
        return jnp.concatenate([bias_block(bta, btb, 2 * p + i, zl, ys) for i in range(2)], axis=1)

    def run(items):
        n = len(items)
        old, sc, w = [None] * n, [None] * n, [None] * n

        def one(i):
            s, p = items[i]
            old[i] = None if first else (m_ref[s, p], l_ref[s, p], acc[s, p, 0], acc[s, p, 1])
            sc[i] = dot(kbuf[slot, s], qz[s, p])

        def two(i):
            s, p = items[i]
            scores = sc[i] + bias(p)
            top = jnp.max(scores, axis=0, keepdims=True)
            if not first:
                top = jnp.maximum(old[i][0], top)
            w[i] = (top, jnp.exp(scores - top).astype(BF16))

        def three(i):
            s, p = items[i]
            top, weights = w[i]
            mixed = dot(vt[slot, s, p], weights)
            total = mixed[2 * HEAD : 2 * HEAD + 1]
            left, right = mixed[:HEAD, :ROWS], mixed[HEAD : 2 * HEAD, ROWS:]
            if not first:
                scale = jnp.exp(old[i][0] - top)
                total = old[i][1] * scale + total
                left = old[i][2] * scale[:, :ROWS] + left
                right = old[i][3] * scale[:, ROWS:] + right
            m_ref[s, p], l_ref[s, p], acc[s, p, 0], acc[s, p, 1] = top, total, left, right

        for t in range(n + 4):
            if t < n:
                one(t)
            if 0 <= t - 2 < n:
                two(t - 2)
            if 0 <= t - 4 < n:
                three(t - 4)

    run([(s, p) for s in range(SEQS) for p in pairs])


def finish(wo, gt, l_ref, acc, held, out, sems):
    copies = []
    for s in range(SEQS):
        parts = []
        for p in range(PAIRS):
            for half in range(2):
                h = 2 * p + half
                total = l_ref[s, p, :, half * ROWS : (half + 1) * ROWS]
                parts.append(acc[s, p, half] / total * gt[s, h * HEAD : (h + 1) * HEAD])
        gated = jnp.concatenate(parts, axis=0).astype(BF16)
        held[s] = dot(gated.T, wo[...]).astype(BF16)
        copies.append(pltpu.make_async_copy(held.at[s], out.at[s], sems.at[s]))
        copies[-1].start()
    for copy in copies:
        copy.wait()


def kernel(
    x_hbm, gain_hbm, wq_hbm, wk_hbm, wv_hbm, wg_hbm, wo_hbm, b_hbm, out,
    x, gain, wq, wk, wv, wg, wo, b,
    xg, bta, btb, wvt, kbuf, vt, qz, gt, m_ref, l_ref, acc,
    local, ready, sent, received,
):
    seq, res = lax.axis_index("seq"), lax.axis_index("res")
    zl, y, xx = seq // (NY * NX), lax.rem(seq // NX, NY), lax.rem(seq, NX)
    zh, core = res // 2, lax.rem(res, 2)

    def at_seq(zl_, y_, x_):
        return (zl_ * (NY * NX) + y_ * NX + x_, res)

    def at_res(zh_, core_):
        return (seq, zh_ * 2 + core_)

    def mod(v, n):
        return lax.rem(v + n, n)

    def y_at(k):
        return mod(y + k, NY)

    z_next, z_prev, z_opp = mod(zh + 1, NZH), mod(zh - 1, NZH), mod(zh + 2, NZH)
    y_next, y_prev = y_at(1), y_at(-1)
    x_next, x_prev, x_opp = mod(xx + 1, NX), mod(xx - 1, NX), mod(xx + 2, NX)
    z_side = (zl, 1 - zl)

    barrier = pltpu.get_barrier_semaphore()
    partners = {
        "zn": (at_res(z_next, core), zh < z_next, 1),
        "zp": (at_res(z_prev, core), zh < z_prev, 0),
        "sib": (at_res(zh, 1 - core), core < 1, 2),
        "yn": (at_seq(zl, y_next, xx), y < y_next, 4),
        "yp": (at_seq(zl, y_prev, xx), y < y_prev, 3),
        "xn": (at_seq(zl, y, x_next), xx < x_next, 6),
        "xp": (at_seq(zl, y, x_prev), xx < x_prev, 5),
        "xo": (at_seq(zl, y, x_opp), xx < x_opp, 7),
        "zl": (at_seq(1 - zl, y, xx), zl < 1, 8),
    }
    slots = {name: i for i, name in enumerate(partners)}
    late = 0
    for dev, early, _ in partners.values():
        late = late + jnp.where(early, 0, 1)

        @pl.when(early)
        def _(dev=dev):
            pl.semaphore_signal(barrier, inc=1, device_id=dev, device_id_type=MESH)

    loads = [
        pltpu.make_async_copy(src, dst, local.at[i])
        for i, (src, dst) in enumerate(
            [(x_hbm, x), (gain_hbm, gain), (b_hbm, b), (wk_hbm, wk), (wv_hbm, wv), (wq_hbm, wq), (wg_hbm, wg), (wo_hbm, wo)]
        )
    ]
    for load in loads:
        load.start()
    @pl.when(late > 0)
    def _():
        pl.semaphore_wait(barrier, late)

    for dev, early, slot in partners.values():

        @pl.when(jnp.logical_not(early))
        def _(dev=dev, slot=slot):
            pl.semaphore_signal(ready.at[slot], inc=1, device_id=dev, device_id_type=MESH)

    loads[0].wait()
    loads[1].wait()
    for s in range(SEQS):
        xg[zh, core, s] = normalise(x[s], gain[...])
    loads[2].wait()
    bta[y, zl, xx] = b[:FIRST]
    btb[xx, zl, y] = b[FIRST:]

    started, greeted, numbers = [], set(), {}

    def copy_of(key, ref, name):
        i = numbers.setdefault(key, len(numbers))
        return pltpu.make_async_remote_copy(
            src_ref=ref, dst_ref=ref, send_sem=sent.at[i], recv_sem=received.at[i],
            device_id=partners[name][0], device_id_type=MESH,
        )

    def greet(name):
        if name not in greeted:
            greeted.add(name)

            @pl.when(partners[name][1])
            def _():
                pl.semaphore_wait(ready.at[slots[name]], 1)

    def send(key, ref, name):
        greet(name)
        copy = copy_of(key, ref, name)
        copy.start()
        started.append(copy)

    def arrive(key, ref):
        copy_of(key, ref, "sib").wait_recv()

    plan = []

    def at(time):
        def add(step):
            plan.append((time, len(plan), step))
            return step

        return add

    across = (("xn", x_prev), ("xp", x_next), ("xo", x_opp))

    @at(0)
    def _():
        send(("bz",), btb.at[xx, zl, y], "zl")
        send(("az",), bta.at[y, zl, xx], "zl")
        for name, _ in across:
            send(("ax", 0, name), bta.at[y, zl, xx], name)

    @at(1.31)
    def _():
        arrive(("az",), bta.at[y, 1 - zl, xx])
        for name, _ in across:
            send(("ax", 1, name), bta.at[y, 1 - zl, xx], name)

    for half in range(2):

        @at(1.5 + 1.3 * half)
        def _(half=half):
            for name, origin in across:
                arrive(("ax", half, name), bta.at[y, z_side[half], origin])
            for name in ("yn", "yp"):
                send(("ay", 0, half, name), bta.at[y, z_side[half]], name)

        for k in range(1, 4):

            @at(TA + 2.2 * (k - 1) + 1.1 * half)
            def _(k=k, half=half):
                for name, step, far in (("yn", -k, 0), ("yp", k, 1)):
                    slab = bta.at[y_at(step), z_side[half]]
                    arrive(("ay", k - 1, half, name), slab)
                    if k < 3 or half == far:
                        send(("ay", k, half, name), slab, name)

    @at(TA + 7.4)
    def _():
        arrive(("ay", 3, 0, "yn"), bta.at[y_at(4), z_side[0]])
        arrive(("ay", 3, 1, "yp"), bta.at[y_at(4), z_side[1]])

    def spread(k):
        for name in ("xn", "xp"):
            send(("bx", k, name), btb.at[xx, :, y_at(k)], name)

    @at(1.3)
    def _():
        arrive(("bz",), btb.at[xx, 1 - zl, y])
        for name in ("yn", "yp"):
            send(("by", 0, name), btb.at[xx, :, y], name)
        spread(0)

    for k in range(1, 4):

        @at(1.3 + TB * k)
        def _(k=k):
            for name, step, far in (("yn", -k, 0), ("yp", k, 1)):
                slab = btb.at[xx, :, y_at(step)]
                arrive(("by", k - 1, name), slab)
                send(("by", k, name), slab if k < 3 else btb.at[xx, z_side[far], y_at(step)], name)
            spread(-k)
            spread(k)

    @at(1.3 + TB * 4)
    def _():
        arrive(("by", 3, "yn"), btb.at[xx, z_side[0], y_at(4)])
        arrive(("by", 3, "yp"), btb.at[xx, z_side[1], y_at(4)])
        spread(4)

    order = (0, -1, 1, -2, 2, -3, 3, 4)
    for i, k in enumerate(order):

        @at(max(2.9 + 0.85 * i, 1.4 + TB * abs(k) + 1.4))
        def _(i=i, k=k):
            arrive(("bx", k, "xn"), btb.at[x_prev, :, y_at(k)])
            arrive(("bx", k, "xp"), btb.at[x_next, :, y_at(k)])
            if i in (0, 1, 4, 5):
                send(("bo", k), btb.at[x_prev, :, y_at(k)], "xn")
            else:
                send(("bo", k), btb.at[x_next, :, y_at(k)], "xp")

    @at(11.9)
    def _():
        for k in order:
            arrive(("bo", k), btb.at[x_opp, :, y_at(k)])

    halves = (slice(0, SEQS // 2), slice(SEQS // 2, SEQS))
    first_half = {"zn": 0, "zp": 1}

    def rows_to(name, when_early):
        early = partners[name][1]
        greeted.add(name)
        copies = [
            copy_of(("xo", name, i), xg.at[zh, core, halves[first_half[name] ^ i]], name) for i in range(2)
        ]

        @pl.when(early if when_early else jnp.logical_not(early))
        def _():
            if when_early:
                pl.semaphore_wait(ready.at[slots[name]], 1)
            for copy in copies:
                copy.start()

        if when_early:
            started.extend(copies)

    at(1.32)(lambda: rows_to("zp", False))
    at(1.33)(lambda: rows_to("zn", False))
    at(0.03)(lambda: send(("xs",), xg.at[zh, core], "sib"))
    at(EN)(lambda: rows_to("zn", True))
    at(EP)(lambda: rows_to("zp", True))

    def rows_from(name, origin, i):
        part = xg.at[origin, core, halves[first_half[name] ^ i]]
        onward = [copy_of(("xt", name, i), part, "sib")]
        if i == 0:
            onward.append(copy_of(("xf", name), part, name))
        started.extend(onward)
        come = copy_of(("xo", name, i), part, "sib")

        def step():
            come.wait_recv()
            for copy in onward:
                copy.start()

        at(TX[i])(lambda: pl.when(zh >= 2)(step))
        at(TL[name][i])(lambda: pl.when(zh < 2)(step))

    for name, origin in (("zn", z_prev), ("zp", z_next)):
        for i in range(2):
            rows_from(name, origin, i)

    def rows_told(name, origin, i):
        arrive(("xt", name, i), xg.at[origin, 1 - core, halves[first_half[name] ^ i]])

    state = (kbuf, vt, qz, bta, btb, m_ref, l_ref, acc)
    pairs = range(PAIRS)

    @at(0.04)
    def _():
        loads[3].wait()
        loads[4].wait()
        wvt[...] = wv[...].T
        ones = jnp.ones((AUG - 2 * HEAD, BLOCK), BF16)
        for slot in range(NZH):
            for s in range(SEQS):
                for p in range(PAIRS):
                    vt[slot, s, p, 2 * HEAD :] = ones

    @at(1.7)
    def _():
        loads[5].wait()
        loads[6].wait()
        query_side(lambda s: xg[zh, core, s], wq, wg, qz, gt)

    at(3.1)(lambda: key_side(xg, zh, core, 0, 0, wk, wvt, kbuf, vt))

    @at(6.1)
    def _():
        arrive(("xs",), xg.at[zh, 1 - core])
        key_side(xg, zh, 1 - core, 1, 0, wk, wvt, kbuf, vt)

    for slot, (name, origin) in enumerate((("zn", z_prev), ("zp", z_next)), start=1):

        @at(14.1)
        def _(slot=slot, origin=origin):
            key_side(xg, origin, core, 0, slot, wk, wvt, kbuf, vt)

        @at(14.2)
        def _(slot=slot, name=name, origin=origin):
            rows_told(name, origin, 0)
            rows_told(name, origin, 1)
            key_side(xg, origin, 1 - core, 1, slot, wk, wvt, kbuf, vt)

    at(15.0)(lambda: attend(0, zh, core, True, pairs, *state))
    at(15.2)(lambda: attend(1, z_prev, core, False, pairs, *state))

    @at(15.3)
    def _():
        for name in ("zn", "zp"):
            part = xg.at[z_opp, core, halves[first_half[name]]]
            arrive(("xf", name), part)
            send(("xu", name), part, "sib")

    at(15.4)(lambda: attend(2, z_next, core, False, pairs, *state))

    @at(15.5)
    def _():
        key_side(xg, z_opp, core, 0, 3, wk, wvt, kbuf, vt)
        for name in ("zn", "zp"):
            arrive(("xu", name), xg.at[z_opp, 1 - core, halves[first_half[name]]])
        key_side(xg, z_opp, 1 - core, 1, 3, wk, wvt, kbuf, vt)

    at(15.6)(lambda: attend(3, z_opp, core, False, pairs, *state))
    loads_left = loads[7]

    for _, _, step in sorted(plan, key=lambda entry: entry[:2]):
        step()
    loads_left.wait()
    finish(wo, gt, l_ref, acc, x, out, local)
    for copy in started:
        copy.wait_send()


def scratch():
    sem = pltpu.SemaphoreType.DMA
    mat = pltpu.VMEM((WIDTH, WIDTH), BF16)
    return [
        pltpu.VMEM((SEQS, ROWS, WIDTH), BF16),
        pltpu.VMEM((1, WIDTH), F32),
        mat, mat, mat, mat, mat,
        pltpu.VMEM((HEADS, 16, ROWS), BF16),
        pltpu.VMEM((NZH, 2, SEQS, ROWS, WIDTH), BF16),
        pltpu.VMEM((NY, NZL, NX, FIRST, 16, ROWS), BF16),
        pltpu.VMEM((NX, NZL, NY, HEADS - FIRST, 16, ROWS), BF16),
        mat,
        pltpu.VMEM((NZH, SEQS, BLOCK, WIDTH), BF16),
        pltpu.VMEM((NZH, SEQS, PAIRS, AUG, BLOCK), BF16),
        pltpu.VMEM((SEQS, PAIRS, WIDTH, BLOCK), BF16),
        pltpu.VMEM((SEQS, WIDTH, ROWS), F32),
        pltpu.VMEM((SEQS, PAIRS, 1, BLOCK), F32),
        pltpu.VMEM((SEQS, PAIRS, 1, BLOCK), F32),
        pltpu.VMEM((SEQS, PAIRS, 2, HEAD, ROWS), F32),
        sem((8,)), pltpu.SemaphoreType.REGULAR((9,)),
        sem((COPIES,)), sem((COPIES,)),
    ]


def on_device(x, gain, wq, wk, wv, wg, wo, b):
    any_space = pl.BlockSpec(memory_space=pltpu.HBM)
    return pl.pallas_call(
        kernel,
        out_shape=jax.ShapeDtypeStruct(x.shape, x.dtype),
        in_specs=[any_space] * 8,
        out_specs=any_space,
        scratch_shapes=scratch(),
        compiler_params=pltpu.CompilerParams(
            collective_id=0, has_side_effects=True, vmem_limit_bytes=63 * 1024 * 1024
        ),
        cost_estimate=pl.CostEstimate(flops=6 * 10**9, bytes_accessed=2 * 10**6, transcendentals=5 * 10**6),
    )(x, gain.reshape(1, -1), wq, wk, wv, wg, wo, jnp.swapaxes(b, 1, 2))


def solution(mesh):
    return jax.shard_map(
        on_device,
        mesh=mesh,
        in_specs=(P("seq", "res", None), P(), P(), P(), P(), P(), P(), P(None, "res", "seq")),
        out_specs=P("seq", "res", None),
        check_vma=False,
    )
```
